32 devices in a mesh: curve: 32 (over z, y, x, core).
Axes of the slice: x: 2, y: 2, z: 4, core: 2. Of those that a mesh axis runs over, the one named last changes fastest.
Arguments:
- vectors: bfloat16 [32768, 128], P('curve'), may hold values from -6 to 6
- near_self: bfloat16 [32768, 512], P('curve'), may hold values from -0.15625 to 0.15625
- near_next: bfloat16 [32768, 512], P('curve'), may hold values from -0.15625 to 0.15625
- leaf_basis: bfloat16 [32768, 256], P('curve'), may hold values from -0.25 to 0.25
- transfer_one: bfloat16 [16384, 256], P('curve'), may hold values from -0.25 to 0.25
- transfer_two: bfloat16 [4096, 256], P('curve'), may hold values from -0.25 to 0.25
- coupling_zero: bfloat16 [16384, 3, 256], P('curve'), may hold values from -0.21875 to 0.21875
- coupling_one: bfloat16 [4096, 3, 256], P('curve'), may hold values from -0.21875 to 0.21875
- coupling_two: bfloat16 [1024, 3, 256], P('curve'), may hold values from -0.21875 to 0.21875
- list_zero: int32 [64, 3], P('curve'), may hold values from 0 to 63, as said below
- list_one: int32 [16, 3], replicated, may hold values from 0 to 15, as said below
- list_two: int32 [4, 3], replicated, may hold values from 0 to 3, as said below
Outputs:
- product: bfloat16 [32768, 128], P('curve')
The draws below stay inside these ranges and needn't reach their ends.
Inputs may be any that keep to these rules, and one draw needn't show every extreme that they name: `list_zero`: row c holds 3 different entries (c + d) mod 64, each d one of -3, -2, 2, 3. `list_one`: row p holds 3 entries (p + d) mod 16 for different d among -3, -2, 2, 3. `list_two`: row q holds 3 entries (q + d) mod 4 for different d among -3, -2, 2, 3.
All inputs are finite; a program needn't handle non-finite values.
Results may differ from the reference program's by a relative error of at most 0.014.
Values may be sent and summed in bfloat16 or wider, within the bound.
A program may use at most 64 MiB of HBM per device.

```python
import jax
import jax.numpy as jnp

M = 512
K = 256
R = 128
SLOTS = 3
LEAVES = 64
CLUSTERS_ONE = 16
CLUSTERS_TWO = 4
ORDER = 32768
N_CURVE = 32


def listed_partners(key, clusters):
    offsets = jnp.array([-3, -2, 2, 3], jnp.int32)
    ranking = jax.random.randint(key, (clusters, 4), 0, 1 << 20) * 4 + jnp.arange(4, dtype=jnp.int32)[None, :]
    picked = jnp.argsort(ranking, axis=1)[:, :SLOTS]
    cluster_ids = jnp.arange(clusters, dtype=jnp.int32)[:, None]
    return ((cluster_ids + offsets[picked]) % clusters).astype(jnp.int32)


def draw_list_zero(key, part):
    return listed_partners(jax.random.fold_in(key, 101), LEAVES)


def draw_list_one(key, part):
    return listed_partners(jax.random.fold_in(key, 202), CLUSTERS_ONE)


def draw_list_two(key, part):
    return listed_partners(jax.random.fold_in(key, 303), CLUSTERS_TWO)


def level_of(rng, extent, cuts, least, high):
    def one(position, shards_of):
        heights = jax.random.uniform(jax.random.fold_in(jax.random.fold_in(rng, 6), position), (shards_of,), jnp.float32, least / len(cuts), high / len(cuts))
        return jnp.repeat(jnp.exp(heights), extent[position] // shards_of).reshape((-1,) + (1,) * (len(extent) - position - 1))

    factor_of = one(*cuts[0])
    for cut in cuts[1:]:
        factor_of = factor_of * one(*cut)
    return factor_of


def centred(own_key, dims, scale, bound, pieces=(), kind=jnp.bfloat16):
    result = scale * jax.random.normal(own_key, dims, jnp.float32)
    if pieces:
        result = result * level_of(own_key, dims, pieces, -0.22, 0.18)
    return jnp.clip(result, -bound, bound).astype(kind)


def setup_inputs(seed: int = 0) -> dict:
    streams_of = jax.random.split(jax.random.key(seed), 13)
    return {
        "vectors": centred(streams_of[0], (ORDER, R), 1.0, 6.0, ((0, 32),)),
        "near_self": centred(streams_of[1], (ORDER, M), (3 * M) ** -0.5, 0.15625, ((0, 32),)),
        "near_next": centred(streams_of[2], (ORDER, M), (3 * M) ** -0.5, 0.15625, ((0, 32),)),
        "leaf_basis": centred(streams_of[3], (ORDER, K), M ** -0.5, 0.25, ((0, 32),)),
        "transfer_one": centred(streams_of[4], (LEAVES * K, K), (2 * K) ** -0.5, 0.25, ((0, 32),)),
        "transfer_two": centred(streams_of[5], (CLUSTERS_ONE * K, K), (2 * K) ** -0.5, 0.25, ((0, 32),)),
        "coupling_zero": centred(streams_of[6], (LEAVES * K, SLOTS, K), (SLOTS * K) ** -0.5, 0.21875, ((0, 32),)),
        "coupling_one": centred(streams_of[7], (CLUSTERS_ONE * K, SLOTS, K), (SLOTS * K) ** -0.5, 0.21875, ((0, 32),)),
        "coupling_two": centred(streams_of[8], (CLUSTERS_TWO * K, SLOTS, K), (SLOTS * K) ** -0.5, 0.21875, ((0, 32),)),
        "list_zero": draw_list_zero(jax.random.fold_in(streams_of[12], 71), 0),
        "list_one": draw_list_one(jax.random.fold_in(streams_of[12], 71), 0),
        "list_two": draw_list_two(jax.random.fold_in(streams_of[12], 71), 0),
    }


def lift(coefficients, transfer, clusters):
    blocks = transfer.reshape(clusters, K, K).astype(jnp.float32)
    terms = jnp.einsum("cab,car->cbr", blocks, coefficients.astype(jnp.float32))
    return terms.reshape(clusters // 4, 4, K, R).sum(axis=1).astype(jnp.bfloat16)


def couple(coefficients, coupling, interaction_rows, clusters):
    blocks = coupling.reshape(clusters, K, SLOTS, K).astype(jnp.float32)
    sources = coefficients.astype(jnp.float32)[interaction_rows]
    return jnp.einsum("casb,csar->cbr", blocks, sources)


def expand(far_terms, parent_terms, transfer, clusters):
    blocks = transfer.reshape(clusters, K, K).astype(jnp.float32)
    spread = jnp.repeat(parent_terms.astype(jnp.float32), 4, axis=0)
    return (far_terms + jnp.einsum("cab,cbr->car", blocks, spread)).astype(jnp.bfloat16)


def reference(vectors, near_self, near_next, leaf_basis, transfer_one, transfer_two, coupling_zero, coupling_one, coupling_two, list_zero, list_one, list_two):
    leaf_clusters = 2 * N_CURVE
    points = vectors.reshape(leaf_clusters, M, R).astype(jnp.float32)
    basis = leaf_basis.reshape(leaf_clusters, M, K).astype(jnp.float32)
    coef_zero = jnp.einsum("cmk,cmr->ckr", basis, points).astype(jnp.bfloat16)
    coef_one = lift(coef_zero, transfer_one, leaf_clusters)
    coef_two = lift(coef_one, transfer_two, leaf_clusters // 4)
    far_zero = couple(coef_zero, coupling_zero, list_zero, leaf_clusters)
    far_one = couple(coef_one, coupling_one, list_one, leaf_clusters // 4)
    far_two = couple(coef_two, coupling_two, list_two, leaf_clusters // 16)
    expansion_two = far_two.astype(jnp.bfloat16)
    expansion_first_level = expand(far_one, expansion_two, transfer_two, leaf_clusters // 4)
    expansion_zero = expand(far_zero, expansion_first_level, transfer_one, leaf_clusters)
    far_field = jnp.einsum("cmk,ckr->cmr", basis, expansion_zero.astype(jnp.float32))
    self_blocks = near_self.reshape(leaf_clusters, M, M).astype(jnp.float32)
    next_blocks = near_next.reshape(leaf_clusters, M, M).astype(jnp.float32)
    near_field = jnp.einsum("cmn,cnr->cmr", self_blocks, points)
    near_field = near_field + jnp.einsum("cmn,cnr->cmr", next_blocks, jnp.roll(points, -1, axis=0))
    near_field = near_field + jnp.roll(jnp.einsum("cmn,cmr->cnr", next_blocks, points), 1, axis=0)
    return (near_field + far_field).astype(jnp.bfloat16).reshape(leaf_clusters * M, R)
```

```python
import functools

import jax
import jax.numpy as jnp
from jax import lax
from jax.experimental import pallas as pl
from jax.experimental.pallas import tpu as pltpu
from jax.sharding import PartitionSpec as P

OFFSETS = (-3, -2, 2, 3)


def mm(a, b):
    return lax.dot_general(a, b, (((1,), (0,)), ((), ())), preferred_element_type=jnp.float32)


def tmm(a, b):
    return lax.dot_general(a, b, (((0,), (0,)), ((), ())), preferred_element_type=jnp.float32)


def partner_offsets(clusters):
    found = []
    for offset in OFFSETS:
        if offset % clusters not in found:
            found.append(offset % clusters)
    return found


def slot_of(listed, own, clusters, distances):
    distance = (listed - own + clusters) % clusters
    slot = jnp.int32(0)
    for index, value in enumerate(distances[1:], 1):
        slot = jnp.where(distance == value, jnp.int32(index), slot)
    return slot


def kernel(
    n,
    sizes,
    x_hbm,
    ns_hbm,
    nn_hbm,
    u_hbm,
    e1_hbm,
    e2_hbm,
    c0_hbm,
    c1_hbm,
    c2_hbm,
    l0,
    l1,
    l2,
    out,
    x,
    ns,
    nn,
    u,
    e1,
    e2,
    c0,
    c1,
    c2,
    win,
    xnext,
    term_out,
    term_in,
    p1,
    p1_out,
    p1_in,
    one,
    one_in,
    f1_out,
    f1_in,
    p2,
    p2_out,
    p2_in,
    two,
    two_in,
    f2,
    f2_out,
    f2_in,
    ex2,
    h,
    g,
    acc,
    load_sem,
    send_sem,
    recv_sem,
):
    bf16, f32 = jnp.bfloat16, jnp.float32
    m, k, half, part = sizes
    pair, group = k // half, k // part
    me = lax.axis_index("curve")
    t = me % pair
    j = me % group
    base = me - j
    sibling = me - t + (t + 1) % pair
    clusters_one, clusters_two = n // pair, n // group
    far_one_d, far_two_d = partner_offsets(clusters_one), partner_offsets(clusters_two)

    loads = {}
    for index, (name, src, dst) in enumerate(
        (
            ("x", x_hbm, x),
            ("u", u_hbm, u),
            ("e1", e1_hbm, e1),
            ("e2", e2_hbm, e2.at[pl.ds(pl.multiple_of(t * half, half), half)]),
            ("nn", nn_hbm, nn),
            ("c2", c2_hbm, c2),
            ("c1", c1_hbm, c1),
            ("ns", ns_hbm, ns),
            ("c0", c0_hbm, c0),
        )
    ):
        loads[name] = pltpu.make_async_copy(src, dst, load_sem.at[index])
        loads[name].start()

    def shifted(distance):
        return (me + distance % n) % n

    def member(distance):
        return base + (j + distance) % group

    peers = [shifted(d) for d in (1, -1, 2, -2)]
    peers += [shifted(d * pair) for d in far_one_d]
    peers += [shifted(d * group) for d in far_two_d]
    peers += [member(d) for d in range(1, group)]
    barrier = pltpu.get_barrier_semaphore()
    for peer in peers:
        pl.semaphore_signal(
            barrier, inc=1, device_id=(peer,), device_id_type=pl.DeviceIdType.MESH
        )
    pl.semaphore_wait(barrier, len(peers))

    started = []

    def send(src, dst, device):
        index = len(started)
        copy = pltpu.make_async_remote_copy(
            src_ref=src,
            dst_ref=dst,
            send_sem=send_sem.at[index],
            recv_sem=recv_sem.at[index],
            device_id=(device,),
            device_id_type=pl.DeviceIdType.MESH,
        )
        copy.start()
        started.append(copy)
        return copy

    own_half = pl.ds(pl.multiple_of(t * half, half), half)
    other_half = pl.ds(pl.multiple_of((t + 1) % pair * half, half), half)
    own_part = pl.ds(pl.multiple_of(j * part, part), part)

    def part_of(distance):
        return pl.ds(pl.multiple_of((j + distance) % group * part, part), part)

    e2_copy = send(e2_hbm, e2.at[own_half], sibling)
    x_copy = send(x_hbm.at[pl.ds(0, m)], xnext, shifted(-1))

    loads["x"].wait()
    loads["u"].wait()
    coefs = []
    for v in range(2):
        coef = tmm(u[pl.ds(v * m, m)], x[pl.ds(v * m, m)]).astype(bf16)
        win[3 + v] = coef
        coefs.append(coef)
    loads["e1"].wait()
    share = tmm(e1[pl.ds(0, k)], coefs[0]) + tmm(e1[pl.ds(k, k)], coefs[1])
    p1[...] = share
    p1_out[...] = share.astype(bf16)
    p1_copy = send(p1_out.at[other_half], p1_in, sibling)
    loads["e2"].wait()
    e2_copy.wait_recv()
    share = tmm(e2[...], share.astype(bf16))
    p2[...] = share
    p2_out[...] = share.astype(bf16)
    p2_copies = [send(p2_out.at[part_of(d)], p2_in.at[d - 1], member(d)) for d in range(1, group)]
    win_copies = [
        send(win.at[pl.ds(3, 2)], win.at[pl.ds(1, 2)], shifted(1)),
        send(win.at[pl.ds(3, 2)], win.at[pl.ds(5, 2)], shifted(-1)),
        send(win.at[4], win.at[0], shifted(2)),
        send(win.at[3], win.at[7], shifted(-2)),
    ]

    p1_copy.wait_recv()
    one[...] = (p1[own_half, :] + p1_in[...].astype(f32)).astype(bf16)
    one_copies = [
        send(one, one_in.at[s], shifted(-d * pair)) for s, d in enumerate(far_one_d)
    ]

    loads["nn"].wait()
    term_out[...] = tmm(nn[pl.ds(m, m)], x[pl.ds(m, m)]).astype(bf16)
    term_copy = send(term_out, term_in, shifted(1))

    total = p2[own_part, :]
    for d in range(1, group):
        p2_copies[d - 1].wait_recv()
        total = total + p2_in[d - 1].astype(f32)
    two[...] = total.astype(bf16)
    two_copies = [
        send(two, two_in.at[s], shifted(-d * group)) for s, d in enumerate(far_two_d)
    ]

    h[pl.ds(0, m)] = mm(u[pl.ds(0, m)], e1[pl.ds(0, k)]).astype(bf16)
    h[pl.ds(m, m)] = mm(u[pl.ds(m, m)], e1[pl.ds(k, k)]).astype(bf16)

    loads["c2"].wait()
    for copy in two_copies:
        copy.wait_recv()
    own_two = me // group
    share = None
    for s in range(c2.shape[0]):
        slot = slot_of(l2[own_two, s], own_two, clusters_two, far_two_d)
        product = tmm(c2[s], two_in[slot])
        share = product if share is None else share + product
    f2[...] = share
    f2_out[...] = share.astype(bf16)
    f2_copies = [send(f2_out.at[part_of(d)], f2_in.at[d - 1], member(d)) for d in range(1, group)]

    loads["ns"].wait()
    acc[pl.ds(0, m)] = (
        mm(ns[pl.ds(0, m)], x[pl.ds(0, m)])
        + mm(nn[pl.ds(0, m)], x[pl.ds(m, m)])
    )
    acc[pl.ds(m, m)] = mm(ns[pl.ds(m, m)], x[pl.ds(m, m)]) + tmm(
        nn[pl.ds(0, m)], x[pl.ds(0, m)]
    )
    g[...] = mm(h[...], e2[...]).astype(bf16)

    total = f2[own_part, :]
    for d in range(1, group):
        f2_copies[d - 1].wait_recv()
        total = total + f2_in[d - 1].astype(f32)
    ex2[own_part, :] = total.astype(bf16)
    ex2_copies = [send(ex2.at[own_part], ex2.at[own_part], member(d)) for d in range(1, group)]

    loads["c1"].wait()
    for copy in one_copies:
        copy.wait_recv()
    own_one = me // pair
    share = None
    for s in range(c1.shape[0]):
        slot = slot_of(l1[s, own_one], own_one, clusters_one, far_one_d)
        product = tmm(c1[s], one_in[slot])
        share = product if share is None else share + product
    f1_out[...] = share.astype(bf16)
    f1_copy = send(f1_out, f1_in, sibling)

    x_copy.wait_recv()
    acc[pl.ds(m, m)] += mm(nn[pl.ds(m, m)], xnext[...])

    f1_copy.wait_recv()
    far_one = (f1_in[...].astype(f32) + share).astype(bf16)
    acc[...] += mm(h[...], far_one)

    term_copy.wait_recv()
    acc[pl.ds(0, m)] += term_in[...].astype(f32)

    loads["c0"].wait()
    for copy in win_copies:
        copy.wait_recv()
    for v in range(2):
        share = None
        for s in range(c0.shape[0]):
            distance = (l0[v, s] - (2 * me + v) + 3 + 2 * n) % (2 * n)
            product = tmm(c0[s, pl.ds(v * k, k)], win[jnp.minimum(v + distance, 7)])
            share = product if share is None else share + product
        acc[pl.ds(v * m, m)] += mm(u[pl.ds(v * m, m)], share.astype(bf16))

    for copy in ex2_copies:
        copy.wait_recv()
    out[...] = (acc[...] + mm(g[...], ex2[...])).astype(bf16)

    for copy in started:
        copy.wait_send()


def per_device(n, x, ns, nn, u, e1, e2, c0, c1, c2, l0, l1, l2):
    bf16, f32 = jnp.bfloat16, jnp.float32
    m, k, r = ns.shape[1], u.shape[1], x.shape[1]
    half, part = e2.shape[0], c2.shape[0]
    group = k // part
    c0, c1, c2 = (jnp.transpose(c, (1, 0, 2)) for c in (c0, c1, c2))
    ones, twos = len(partner_offsets(n * half // k)), len(partner_offsets(n // group))
    copies = 2 + 1 + 3 * (group - 1) + 4 + ones + twos + 1 + 1
    V = pltpu.VMEM
    scratch = [
        V(x.shape, bf16),
        V(ns.shape, bf16),
        V(nn.shape, bf16),
        V(u.shape, bf16),
        V(e1.shape, bf16),
        V((k, k), bf16),
        V(c0.shape, bf16),
        V(c1.shape, bf16),
        V(c2.shape, bf16),
        V((8, k, r), bf16),
        V((m, r), bf16),
        V((m, r), bf16),
        V((m, r), bf16),
        V((k, r), f32),
        V((k, r), bf16),
        V((half, r), bf16),
        V((half, r), bf16),
        V((ones, half, r), bf16),
        V((k, r), bf16),
        V((k, r), bf16),
        V((k, r), f32),
        V((k, r), bf16),
        V((group - 1, part, r), bf16),
        V((part, r), bf16),
        V((twos, part, r), bf16),
        V((k, r), f32),
        V((k, r), bf16),
        V((group - 1, part, r), bf16),
        V((k, r), bf16),
        V((2 * m, k), bf16),
        V((2 * m, k), bf16),
        V((2 * m, r), f32),
        pltpu.SemaphoreType.DMA((9,)),
        pltpu.SemaphoreType.DMA((copies,)),
        pltpu.SemaphoreType.DMA((copies,)),
    ]
    return pl.pallas_call(
        functools.partial(kernel, n, (m, k, half, part)),
        out_shape=jax.ShapeDtypeStruct(x.shape, bf16),
        in_specs=[pl.BlockSpec(memory_space=pltpu.HBM)] * 9
        + [pl.BlockSpec(memory_space=pltpu.SMEM)] * 3,
        out_specs=pl.BlockSpec(memory_space=pltpu.VMEM),
        scratch_shapes=scratch,
        compiler_params=pltpu.CompilerParams(
            collective_id=0, has_side_effects=True, vmem_limit_bytes=62 << 20
        ),
    )(x, ns, nn, u, e1, e2, c0, c1, c2, l0, l1.T, l2)


def solution(mesh):
    rows, cubes = P("curve", None), P("curve", None, None)
    return jax.shard_map(
        functools.partial(per_device, mesh.shape["curve"]),
        mesh=mesh,
        in_specs=(rows,) * 6 + (cubes,) * 3 + (rows, P(), P()),
        out_specs=rows,
        check_vma=False,
    )
```

```python
import functools

import jax
import jax.numpy as jnp
from jax import lax
from jax.experimental import pallas as pl
from jax.experimental.pallas import tpu as pltpu
from jax.sharding import PartitionSpec as P

OFFSETS = (-3, -2, 2, 3)


def mm(a, b):
    return lax.dot_general(a, b, (((1,), (0,)), ((), ())), preferred_element_type=jnp.float32)


def tmm(a, b):
    return lax.dot_general(a, b, (((0,), (0,)), ((), ())), preferred_element_type=jnp.float32)


def partner_offsets(clusters):
    found = []
    for offset in OFFSETS:
        if offset % clusters not in found:
            found.append(offset % clusters)
    return found


def slot_of(listed, own, clusters, distances):
    distance = (listed - own + clusters) % clusters
    slot = jnp.int32(0)
    for index, value in enumerate(distances[1:], 1):
        slot = jnp.where(distance == value, jnp.int32(index), slot)
    return slot


def kernel(
    n,
    sizes,
    x_hbm,
    ns_hbm,
    nn_hbm,
    u_hbm,
    e1_hbm,
    e2_hbm,
    c0_hbm,
    c1_hbm,
    c2_hbm,
    l0,
    l1,
    l2,
    out,
    x,
    ns,
    nn,
    u,
    e1,
    e2,
    c0,
    c1,
    c2,
    win,
    xnext,
    term_out,
    term_in,
    p1,
    p1_out,
    p1_in,
    one,
    one_in,
    f1_out,
    f1_in,
    p2,
    p2_out,
    p2_in,
    two,
    two_in,
    f2,
    f2_out,
    f2_in,
    ex2,
    h,
    g,
    acc,
    load_sem,
    send_sem,
    recv_sem,
):
    bf16, f32 = jnp.bfloat16, jnp.float32
    m, k, half, part = sizes
    pair, group = k // half, k // part
    me = lax.axis_index("curve")
    t = me % pair
    j = me % group
    base = me - j
    sibling = me - t + (t + 1) % pair
    clusters_one, clusters_two = n // pair, n // group
    far_one_d, far_two_d = partner_offsets(clusters_one), partner_offsets(clusters_two)

    loads = {}
    for index, (name, src, dst) in enumerate(
        (
            ("x", x_hbm, x),
            ("u", u_hbm, u),
            ("e1", e1_hbm, e1),
            ("e2", e2_hbm, e2.at[pl.ds(pl.multiple_of(t * half, half), half)]),
            ("nn", nn_hbm, nn),
            ("c2", c2_hbm, c2),
            ("c1", c1_hbm, c1),
            ("ns", ns_hbm, ns),
            ("c0", c0_hbm, c0),
        )
    ):
        loads[name] = pltpu.make_async_copy(src, dst, load_sem.at[index])
        loads[name].start()

    def shifted(distance):
        return (me + distance % n) % n

    def member(distance):
        return base + (j + distance) % group

    peers = [shifted(d) for d in (1, -1, 2, -2)]
    peers += [shifted(d * pair) for d in far_one_d]
    peers += [shifted(d * group) for d in far_two_d]
    peers += [member(d) for d in range(1, group)]
    barrier = pltpu.get_barrier_semaphore()
    for peer in peers:
        pl.semaphore_signal(
            barrier, inc=1, device_id=(peer,), device_id_type=pl.DeviceIdType.MESH
        )
    pl.semaphore_wait(barrier, len(peers))

    started = []

    def send(src, dst, device):
        index = len(started)
        copy = pltpu.make_async_remote_copy(
            src_ref=src,
            dst_ref=dst,
            send_sem=send_sem.at[index],
            recv_sem=recv_sem.at[index],
            device_id=(device,),
            device_id_type=pl.DeviceIdType.MESH,
        )
        copy.start()
        started.append(copy)
        return copy

    odd = me % 2
    own_half = pl.ds(pl.multiple_of(t * half, half), half)
    other_half = pl.ds(pl.multiple_of((t + 1) % pair * half, half), half)
    own_part = pl.ds(pl.multiple_of(j * part, part), part)

    def part_of(distance):
        return pl.ds(pl.multiple_of((j + distance) % group * part, part), part)

    e2_copy = send(e2_hbm, e2.at[own_half], sibling)

    loads["x"].wait()
    loads["u"].wait()
    coefs = []
    for v in range(2):
        coef = tmm(u[pl.ds(v * m, m)], x[pl.ds(v * m, m)]).astype(bf16)
        win[3 + v] = coef
        coefs.append(coef)
    loads["e1"].wait()
    share = tmm(e1[pl.ds(0, k)], coefs[0]) + tmm(e1[pl.ds(k, k)], coefs[1])
    p1[...] = share
    p1_out[...] = share.astype(bf16)
    p1_copy = send(p1_out.at[other_half], p1_in, sibling)
    loads["e2"].wait()
    e2_copy.wait_recv()
    share = tmm(e2[...], share.astype(bf16))
    p2[...] = share
    p2_out[...] = share.astype(bf16)
    p2_copies = [send(p2_out.at[part_of(d)], p2_in.at[d - 1], member(d)) for d in range(1, group)]


    p1_copy.wait_recv()
    one[...] = (p1[own_half, :] + p1_in[...].astype(f32)).astype(bf16)
    one_copies = [
        send(one, one_in.at[s], shifted(-d * pair)) for s, d in enumerate(far_one_d)
    ]

    loads["nn"].wait()
    term_out[...] = tmm(nn[pl.ds(m, m)], x[pl.ds(m, m)]).astype(bf16)
    term_copy = send(term_out, term_in, shifted(1))

    total = p2[own_part, :]
    for d in range(1, group):
        p2_copies[d - 1].wait_recv()
        total = total + p2_in[d - 1].astype(f32)
    two[...] = total.astype(bf16)
    two_copies = [
        send(two, two_in.at[s], shifted(-d * group)) for s, d in enumerate(far_two_d)
    ]

    win_copies = [
        send(win.at[pl.ds(3, 2)], win.at[pl.ds(1, 2)], shifted(1)),
        send(win.at[pl.ds(3, 2)], win.at[pl.ds(5, 2)], shifted(-1)),
        send(win.at[4 - odd], win.at[7 * odd], (me + n + 2 - 4 * odd) % n),
    ]

    h[pl.ds(0, m)] = mm(u[pl.ds(0, m)], e1[pl.ds(0, k)]).astype(bf16)
    h[pl.ds(m, m)] = mm(u[pl.ds(m, m)], e1[pl.ds(k, k)]).astype(bf16)

    loads["c2"].wait()
    for copy in two_copies:
        copy.wait_recv()
    own_two = me // group
    share = None
    for s in range(c2.shape[0]):
        slot = slot_of(l2[own_two, s], own_two, clusters_two, far_two_d)
        product = tmm(c2[s], two_in[slot])
        share = product if share is None else share + product
    f2[...] = share
    f2_out[...] = share.astype(bf16)
    f2_copies = [send(f2_out.at[part_of(d)], f2_in.at[d - 1], member(d)) for d in range(1, group)]

    x_copy = send(x_hbm.at[pl.ds(0, m)], xnext, shifted(-1))
    loads["ns"].wait()
    acc[pl.ds(0, m)] = (
        mm(ns[pl.ds(0, m)], x[pl.ds(0, m)])
        + mm(nn[pl.ds(0, m)], x[pl.ds(m, m)])
    )
    acc[pl.ds(m, m)] = mm(ns[pl.ds(m, m)], x[pl.ds(m, m)]) + tmm(
        nn[pl.ds(0, m)], x[pl.ds(0, m)]
    )
    g[...] = mm(h[...], e2[...]).astype(bf16)

    total = f2[own_part, :]
    for d in range(1, group):
        f2_copies[d - 1].wait_recv()
        total = total + f2_in[d - 1].astype(f32)
    ex2[own_part, :] = total.astype(bf16)
    ex2_copies = [send(ex2.at[own_part], ex2.at[own_part], member(d)) for d in range(1, group)]

    win_copies[0].wait_recv()
    win_copies[1].wait_recv()
    pass_copy = send(win.at[2 + 3 * odd], win.at[7 * odd], me + 1 - 2 * odd)

    loads["c1"].wait()
    for copy in one_copies:
        copy.wait_recv()
    own_one = me // pair
    share = None
    for s in range(c1.shape[0]):
        slot = slot_of(l1[s, own_one], own_one, clusters_one, far_one_d)
        product = tmm(c1[s], one_in[slot])
        share = product if share is None else share + product
    f1_out[...] = share.astype(bf16)
    f1_copy = send(f1_out, f1_in, sibling)

    x_copy.wait_recv()
    acc[pl.ds(m, m)] += mm(nn[pl.ds(m, m)], xnext[...])

    f1_copy.wait_recv()
    far_one = (f1_in[...].astype(f32) + share).astype(bf16)
    acc[...] += mm(h[...], far_one)

    term_copy.wait_recv()
    acc[pl.ds(0, m)] += term_in[...].astype(f32)

    loads["c0"].wait()
    for copy in (win_copies[2], pass_copy):
        copy.wait_recv()
    for v in range(2):
        share = None
        for s in range(c0.shape[0]):
            distance = (l0[v, s] - (2 * me + v) + 3 + 2 * n) % (2 * n)
            product = tmm(c0[s, pl.ds(v * k, k)], win[jnp.minimum(v + distance, 7)])
            share = product if share is None else share + product
        acc[pl.ds(v * m, m)] += mm(u[pl.ds(v * m, m)], share.astype(bf16))

    for copy in ex2_copies:
        copy.wait_recv()
    out[...] = (acc[...] + mm(g[...], ex2[...])).astype(bf16)

    for copy in started:
        copy.wait_send()


def per_device(n, x, ns, nn, u, e1, e2, c0, c1, c2, l0, l1, l2):
    bf16, f32 = jnp.bfloat16, jnp.float32
    m, k, r = ns.shape[1], u.shape[1], x.shape[1]
    half, part = e2.shape[0], c2.shape[0]
    group = k // part
    c0, c1, c2 = (jnp.transpose(c, (1, 0, 2)) for c in (c0, c1, c2))
    ones, twos = len(partner_offsets(n * half // k)), len(partner_offsets(n // group))
    copies = 2 + 1 + 3 * (group - 1) + 4 + ones + twos + 1 + 1
    V = pltpu.VMEM
    scratch = [
        V(x.shape, bf16),
        V(ns.shape, bf16),
        V(nn.shape, bf16),
        V(u.shape, bf16),
        V(e1.shape, bf16),
        V((k, k), bf16),
        V(c0.shape, bf16),
        V(c1.shape, bf16),
        V(c2.shape, bf16),
        V((8, k, r), bf16),
        V((m, r), bf16),
        V((m, r), bf16),
        V((m, r), bf16),
        V((k, r), f32),
        V((k, r), bf16),
        V((half, r), bf16),
        V((half, r), bf16),
        V((ones, half, r), bf16),
        V((k, r), bf16),
        V((k, r), bf16),
        V((k, r), f32),
        V((k, r), bf16),
        V((group - 1, part, r), bf16),
        V((part, r), bf16),
        V((twos, part, r), bf16),
        V((k, r), f32),
        V((k, r), bf16),
        V((group - 1, part, r), bf16),
        V((k, r), bf16),
        V((2 * m, k), bf16),
        V((2 * m, k), bf16),
        V((2 * m, r), f32),
        pltpu.SemaphoreType.DMA((9,)),
        pltpu.SemaphoreType.DMA((copies,)),
        pltpu.SemaphoreType.DMA((copies,)),
    ]
    return pl.pallas_call(
        functools.partial(kernel, n, (m, k, half, part)),
        out_shape=jax.ShapeDtypeStruct(x.shape, bf16),
        in_specs=[pl.BlockSpec(memory_space=pltpu.HBM)] * 9
        + [pl.BlockSpec(memory_space=pltpu.SMEM)] * 3,
        out_specs=pl.BlockSpec(memory_space=pltpu.VMEM),
        scratch_shapes=scratch,
        compiler_params=pltpu.CompilerParams(
            collective_id=0, has_side_effects=True, vmem_limit_bytes=62 << 20
        ),
    )(x, ns, nn, u, e1, e2, c0, c1, c2, l0, l1.T, l2)


def solution(mesh):
    rows, cubes = P("curve", None), P("curve", None, None)
    return jax.shard_map(
        functools.partial(per_device, mesh.shape["curve"]),
        mesh=mesh,
        in_specs=(rows,) * 6 + (cubes,) * 3 + (rows, P(), P()),
        out_specs=rows,
        check_vma=False,
    )
```

```python
import functools

import jax
import jax.numpy as jnp
from jax import lax
from jax.experimental import pallas as pl
from jax.experimental.pallas import tpu as pltpu
from jax.sharding import PartitionSpec as P

OFFSETS = (-3, -2, 2, 3)


def mm(a, b):
    return lax.dot_general(a, b, (((1,), (0,)), ((), ())), preferred_element_type=jnp.float32)


def tmm(a, b):
    return lax.dot_general(a, b, (((0,), (0,)), ((), ())), preferred_element_type=jnp.float32)


def partner_offsets(clusters):
    found = []
    for offset in OFFSETS:
        if offset % clusters not in found:
            found.append(offset % clusters)
    return found


def slot_of(listed, own, clusters, distances):
    distance = (listed - own + clusters) % clusters
    slot = jnp.int32(0)
    for index, value in enumerate(distances[1:], 1):
        slot = jnp.where(distance == value, jnp.int32(index), slot)
    return slot


def kernel(
    n,
    sizes,
    x_hbm,
    ns_hbm,
    nn_hbm,
    u_hbm,
    e1_hbm,
    e2_hbm,
    c0_hbm,
    c1_hbm,
    c2_hbm,
    l0,
    l1,
    l2,
    out,
    x,
    ns,
    nn,
    u,
    e1,
    e2,
    c0,
    c1,
    c2,
    win,
    xnext,
    term_out,
    term_in,
    p1,
    p1_out,
    p1_in,
    one,
    one_in,
    f1_out,
    f1_in,
    p2,
    p2_out,
    p2_in,
    two,
    two_in,
    f2,
    f2_out,
    f2_in,
    ex2,
    h,
    g,
    acc,
    load_sem,
    send_sem,
    recv_sem,
):
    bf16, f32 = jnp.bfloat16, jnp.float32
    m, k, half, part = sizes
    pair, group = k // half, k // part
    me = lax.axis_index("curve")
    t = me % pair
    j = me % group
    base = me - j
    sibling = me - t + (t + 1) % pair
    clusters_one, clusters_two = n // pair, n // group
    far_one_d, far_two_d = partner_offsets(clusters_one), partner_offsets(clusters_two)

    loads = {}
    for index, (name, src, dst) in enumerate(
        (
            ("x", x_hbm, x),
            ("u", u_hbm, u),
            ("e1", e1_hbm, e1),
            ("e2", e2_hbm, e2.at[pl.ds(pl.multiple_of(t * half, half), half)]),
            ("nn", nn_hbm, nn),
            ("c2", c2_hbm, c2),
            ("c1", c1_hbm, c1),
            ("ns", ns_hbm, ns),
            ("c0", c0_hbm, c0),
        )
    ):
        loads[name] = pltpu.make_async_copy(src, dst, load_sem.at[index])
        loads[name].start()

    def shifted(distance):
        return (me + distance % n) % n

    def member(distance):
        return base + (j + distance) % group

    peers = [shifted(d) for d in (1, -1, 2, -2)]
    peers += [shifted(d * pair) for d in far_one_d]
    peers += [shifted(d * group) for d in far_two_d]
    peers += [member(d) for d in range(1, group)]
    barrier = pltpu.get_barrier_semaphore()
    for peer in peers:
        pl.semaphore_signal(
            barrier, inc=1, device_id=(peer,), device_id_type=pl.DeviceIdType.MESH
        )
    pl.semaphore_wait(barrier, len(peers))

    started = []

    def send(src, dst, device):
        index = len(started)
        copy = pltpu.make_async_remote_copy(
            src_ref=src,
            dst_ref=dst,
            send_sem=send_sem.at[index],
            recv_sem=recv_sem.at[index],
            device_id=(device,),
            device_id_type=pl.DeviceIdType.MESH,
        )
        copy.start()
        started.append(copy)
        return copy

    odd = me % 2
    own_half = pl.ds(pl.multiple_of(t * half, half), half)
    other_half = pl.ds(pl.multiple_of((t + 1) % pair * half, half), half)
    own_part = pl.ds(pl.multiple_of(j * part, part), part)

    def part_of(distance):
        return pl.ds(pl.multiple_of((j + distance) % group * part, part), part)

    e2_copy = send(e2_hbm, e2.at[own_half], sibling)

    loads["x"].wait()
    loads["u"].wait()
    coefs = []
    for v in range(2):
        coef = tmm(u[pl.ds(v * m, m)], x[pl.ds(v * m, m)]).astype(bf16)
        win[3 + v] = coef
        coefs.append(coef)
    loads["e1"].wait()
    share = tmm(e1[pl.ds(0, k)], coefs[0]) + tmm(e1[pl.ds(k, k)], coefs[1])
    p1[...] = share
    p1_out[...] = share.astype(bf16)
    p1_copy = send(p1_out.at[other_half], p1_in, sibling)
    loads["e2"].wait()
    e2_copy.wait_recv()
    share = tmm(e2[...], share.astype(bf16))
    p2[...] = share
    p2_out[...] = share.astype(bf16)
    p2_copies = [send(p2_out.at[part_of(d)], p2_in.at[d - 1], member(d)) for d in range(1, group)]
    win_copies = [
        send(win.at[pl.ds(3, 2)], win.at[pl.ds(1, 2)], shifted(1)),
        send(win.at[pl.ds(3, 2)], win.at[pl.ds(5, 2)], shifted(-1)),
        send(win.at[4 - odd], win.at[7 * odd], (me + n + 2 - 4 * odd) % n),
    ]


    p1_copy.wait_recv()
    one[...] = (p1[own_half, :] + p1_in[...].astype(f32)).astype(bf16)
    one_copies = [
        send(one, one_in.at[s], shifted(-d * pair)) for s, d in enumerate(far_one_d)
    ]

    loads["nn"].wait()
    term_out[...] = tmm(nn[pl.ds(m, m)], x[pl.ds(m, m)]).astype(bf16)
    term_copy = send(term_out, term_in, shifted(1))

    total = p2[own_part, :]
    for d in range(1, group):
        p2_copies[d - 1].wait_recv()
        total = total + p2_in[d - 1].astype(f32)
    two[...] = total.astype(bf16)
    two_copies = [
        send(two, two_in.at[s], shifted(-d * group)) for s, d in enumerate(far_two_d)
    ]

    h[pl.ds(0, m)] = mm(u[pl.ds(0, m)], e1[pl.ds(0, k)]).astype(bf16)
    h[pl.ds(m, m)] = mm(u[pl.ds(m, m)], e1[pl.ds(k, k)]).astype(bf16)

    loads["c2"].wait()
    for copy in two_copies:
        copy.wait_recv()
    own_two = me // group
    share = None
    for s in range(c2.shape[0]):
        slot = slot_of(l2[own_two, s], own_two, clusters_two, far_two_d)
        product = tmm(c2[s], two_in[slot])
        share = product if share is None else share + product
    f2[...] = share
    f2_out[...] = share.astype(bf16)
    f2_copies = [send(f2_out.at[part_of(d)], f2_in.at[d - 1], member(d)) for d in range(1, group)]

    x_copy = send(x_hbm.at[pl.ds(0, m)], xnext, shifted(-1))
    loads["ns"].wait()
    acc[pl.ds(0, m)] = (
        mm(ns[pl.ds(0, m)], x[pl.ds(0, m)])
        + mm(nn[pl.ds(0, m)], x[pl.ds(m, m)])
    )
    acc[pl.ds(m, m)] = mm(ns[pl.ds(m, m)], x[pl.ds(m, m)]) + tmm(
        nn[pl.ds(0, m)], x[pl.ds(0, m)]
    )
    g[...] = mm(h[...], e2[...]).astype(bf16)

    total = f2[own_part, :]
    for d in range(1, group):
        f2_copies[d - 1].wait_recv()
        total = total + f2_in[d - 1].astype(f32)
    ex2[own_part, :] = total.astype(bf16)
    ex2_copies = [send(ex2.at[own_part], ex2.at[own_part], member(d)) for d in range(1, group)]

    win_copies[0].wait_recv()
    win_copies[1].wait_recv()
    pass_copy = send(win.at[2 + 3 * odd], win.at[7 * odd], me + 1 - 2 * odd)

    loads["c1"].wait()
    for copy in one_copies:
        copy.wait_recv()
    own_one = me // pair
    share = None
    for s in range(c1.shape[0]):
        slot = slot_of(l1[s, own_one], own_one, clusters_one, far_one_d)
        product = tmm(c1[s], one_in[slot])
        share = product if share is None else share + product
    f1_out[...] = share.astype(bf16)
    f1_copy = send(f1_out, f1_in, sibling)

    x_copy.wait_recv()
    acc[pl.ds(m, m)] += mm(nn[pl.ds(m, m)], xnext[...])

    f1_copy.wait_recv()
    far_one = (f1_in[...].astype(f32) + share).astype(bf16)
    acc[...] += mm(h[...], far_one)

    term_copy.wait_recv()
    acc[pl.ds(0, m)] += term_in[...].astype(f32)

    loads["c0"].wait()
    for copy in (win_copies[2], pass_copy):
        copy.wait_recv()
    for v in range(2):
        share = None
        for s in range(c0.shape[0]):
            distance = (l0[v, s] - (2 * me + v) + 3 + 2 * n) % (2 * n)
            product = tmm(c0[s, pl.ds(v * k, k)], win[jnp.minimum(v + distance, 7)])
            share = product if share is None else share + product
        acc[pl.ds(v * m, m)] += mm(u[pl.ds(v * m, m)], share.astype(bf16))

    for copy in ex2_copies:
        copy.wait_recv()
    out[...] = (acc[...] + mm(g[...], ex2[...])).astype(bf16)

    for copy in started:
        copy.wait_send()


def per_device(n, x, ns, nn, u, e1, e2, c0, c1, c2, l0, l1, l2):
    bf16, f32 = jnp.bfloat16, jnp.float32
    m, k, r = ns.shape[1], u.shape[1], x.shape[1]
    half, part = e2.shape[0], c2.shape[0]
    group = k // part
    c0, c1, c2 = (jnp.transpose(c, (1, 0, 2)) for c in (c0, c1, c2))
    ones, twos = len(partner_offsets(n * half // k)), len(partner_offsets(n // group))
    copies = 2 + 1 + 3 * (group - 1) + 4 + ones + twos + 1 + 1
    V = pltpu.VMEM
    scratch = [
        V(x.shape, bf16),
        V(ns.shape, bf16),
        V(nn.shape, bf16),
        V(u.shape, bf16),
        V(e1.shape, bf16),
        V((k, k), bf16),
        V(c0.shape, bf16),
        V(c1.shape, bf16),
        V(c2.shape, bf16),
        V((8, k, r), bf16),
        V((m, r), bf16),
        V((m, r), bf16),
        V((m, r), bf16),
        V((k, r), f32),
        V((k, r), bf16),
        V((half, r), bf16),
        V((half, r), bf16),
        V((ones, half, r), bf16),
        V((k, r), bf16),
        V((k, r), bf16),
        V((k, r), f32),
        V((k, r), bf16),
        V((group - 1, part, r), bf16),
        V((part, r), bf16),
        V((twos, part, r), bf16),
        V((k, r), f32),
        V((k, r), bf16),
        V((group - 1, part, r), bf16),
        V((k, r), bf16),
        V((2 * m, k), bf16),
        V((2 * m, k), bf16),
        V((2 * m, r), f32),
        pltpu.SemaphoreType.DMA((9,)),
        pltpu.SemaphoreType.DMA((copies,)),
        pltpu.SemaphoreType.DMA((copies,)),
    ]
    return pl.pallas_call(
        functools.partial(kernel, n, (m, k, half, part)),
        out_shape=jax.ShapeDtypeStruct(x.shape, bf16),
        in_specs=[pl.BlockSpec(memory_space=pltpu.HBM)] * 9
        + [pl.BlockSpec(memory_space=pltpu.SMEM)] * 3,
        out_specs=pl.BlockSpec(memory_space=pltpu.VMEM),
        scratch_shapes=scratch,
        compiler_params=pltpu.CompilerParams(
            collective_id=0, has_side_effects=True, vmem_limit_bytes=62 << 20
        ),
    )(x, ns, nn, u, e1, e2, c0, c1, c2, l0, l1.T, l2)


def solution(mesh):
    rows, cubes = P("curve", None), P("curve", None, None)
    return jax.shard_map(
        functools.partial(per_device, mesh.shape["curve"]),
        mesh=mesh,
        in_specs=(rows,) * 6 + (cubes,) * 3 + (rows, P(), P()),
        out_specs=rows,
        check_vma=False,
    )
```
